512 devices in a mesh: rep: 32 (over z_lo, x, core), fsdp: 16 (over y, z_hi).
Axes of the slice: x: 4, y: 4, z: 16 (z_hi: 4, z_lo: 4; z = z_hi * 4 + z_lo), core: 2. Of those that a mesh axis runs over, the one named last changes fastest.
Arguments:
- tokens: bfloat16 [32, 4096, 7168], P('rep', 'fsdp'), may hold values from -6 to 6
- cotangent: bfloat16 [32, 4096, 112], P('rep', 'fsdp'), may hold values from -6 to 6
- params: float32 [32, 802816], P('rep', 'fsdp'), may hold values from -0.0625 to 0.0625
- first_moment: float32 [32, 802816], P('rep', 'fsdp'), may hold values from -30 to 30
- second_moment: float32 [32, 802816], P('rep', 'fsdp'), may hold values from 100 to 1000
- mass: float32 [32], P('rep'), may hold values from 0.5 to 2
- step_index: int32 [1], replicated, may hold values from 0 to 999
Outputs:
- new_params: float32 [32, 802816], P('rep', 'fsdp')
- new_first: float32 [32, 802816], P('rep', 'fsdp')
- new_second: float32 [32, 802816], P('rep', 'fsdp')
- new_mass: float32 [32], P('rep')
The draws below stay inside these ranges and needn't reach their ends.
All inputs are finite; a program needn't handle non-finite values.
Results may differ from the reference program's by a relative error of at most 0.017.
Values may be sent and summed in bfloat16 or wider, within the bound.
No kernel may reach another device: no remote copies, remote signals or barrier semaphores. Data moves between devices by JAX's collectives and lax.ppermute only.
A program may use at most 64 MiB of HBM per device.

```python
import math
import jax
import jax.numpy as jnp
from jax import lax

D = 7168
HEAD = 112
TOK_DEV = 256
STEPS = 2
TOK_REP = 4096
PARAMS = 802816
N_REP = 32
N_FSDP = 16


def block_scale(key, dims, pieces, smallest, largest):
    loudness = 1.0
    for dim, shards_of in pieces:
        draws = jax.random.uniform(jax.random.fold_in(jax.random.fold_in(key, 6), dim), (shards_of,), jnp.float32, smallest / len(pieces), largest / len(pieces))
        loudness = loudness * jnp.repeat(jnp.exp(draws), dims[dim] // shards_of).reshape((-1,) + (1,) * (len(dims) - 1 - dim))
    return loudness


def scatter_about(stream_key, extent, scale, most, shards=(), held_as=jnp.bfloat16):
    drawn = scale * jax.random.normal(stream_key, extent, jnp.float32)
    if shards:
        drawn = drawn * block_scale(stream_key, extent, shards, -0.22, 0.18)
    return jnp.clip(drawn, -most, most).astype(held_as)


def setup_inputs(seed: int = 0) -> dict:
    splits = jax.random.split(jax.random.key(seed), 8)
    tokens = scatter_about(splits[0], (N_REP, TOK_REP, D), 1.0, 6.0, ((0, 32), (1, 16)))
    cotangent = scatter_about(splits[1], (N_REP, TOK_REP, HEAD), 1.0, 6.0, ((0, 32), (1, 16)))
    params = scatter_about(splits[2], (N_REP, PARAMS), D ** -0.5, 0.0625, ((0, 32), (1, 16)), jnp.float32)
    first_moment = scatter_about(splits[3], (N_REP, PARAMS), 5.0, 30.0, ((0, 32), (1, 16)), jnp.float32)
    second_moment = jnp.clip(jnp.exp(math.log(1000.0) - 2.3025851 * jax.random.uniform(splits[4], (N_REP, PARAMS), jnp.float32) ** block_scale(splits[4], (N_REP, PARAMS), ((0, 32), (1, 16)), -0.2, 0.2)), 100.0, 1000.0)
    mass = jnp.clip(jnp.exp(math.log(2.0) - 1.3862944 * jax.random.uniform(splits[5], (N_REP,), jnp.float32) ** block_scale(splits[5], (N_REP,), ((0, 32),), -0.2, 0.2)), 0.5, 2.0)
    step_index = jax.random.randint(splits[6], (1,), 0, 1000).astype(jnp.int32)
    return dict(tokens=tokens, cotangent=cotangent, params=params, first_moment=first_moment, second_moment=second_moment, mass=mass, step_index=step_index)


BETA_ONE = 0.9
BETA_TWO = 0.95
ADAM_EPS = 1e-08
RATE = 0.01

def layer_norm(block):
    values = block.astype(jnp.float32)
    center = lax.optimization_barrier(jnp.mean(values, axis=-1, keepdims=True))
    spread = lax.optimization_barrier(jnp.mean((values - center) ** 2, axis=-1, keepdims=True))
    return ((values - center) * lax.rsqrt(spread + 1e-05)).astype(jnp.bfloat16)

def partial_grad(normed, cotangent, value_proj):
    preact = jnp.dot(normed, value_proj, preferred_element_type=jnp.float32)
    sigmoid_val = jax.nn.sigmoid(preact)
    head_grad = (cotangent.astype(jnp.float32) * sigmoid_val * (1.0 + preact * (1.0 - sigmoid_val))).astype(jnp.bfloat16)
    grad_value = lax.dot_general(normed, head_grad, (((0,), (0,)), ((), ())), preferred_element_type=jnp.float32)
    return grad_value.reshape(-1)

def reference(tokens, cotangent, params, first_moment, second_moment, mass, step_index):
    levels = N_REP.bit_length() - 1
    normed_all = lax.map(layer_norm, tokens)
    for section in range(STEPS):
        compute = (params / mass[:, None]).astype(jnp.bfloat16)

        def replica_grad(payload):
            normed_rep, cot_rep, flat_params = payload
            value_proj = flat_params.reshape(D, HEAD)
            normed_blocks = normed_rep.reshape(N_FSDP, TOK_DEV, D)
            cot_blocks = cot_rep.reshape(N_FSDP, TOK_DEV, HEAD)

            def add_block(running, blocks):
                term = partial_grad(blocks[0], blocks[1], value_proj).astype(jnp.bfloat16)
                return (running + lax.optimization_barrier(term).astype(jnp.float32), None)
            running, unused = lax.scan(add_block, jnp.zeros((PARAMS,), jnp.float32), (normed_blocks, cot_blocks))
            return running
        grads = lax.map(replica_grad, (normed_all, cotangent, compute))
        first_moment = BETA_ONE * first_moment + (1.0 - BETA_ONE) * grads
        second_moment = BETA_TWO * second_moment + (1.0 - BETA_TWO) * grads * grads
        step_count = (step_index[0] + section + 1).astype(jnp.float32)
        update = first_moment / (1.0 - jnp.power(BETA_ONE, step_count)) / (jnp.sqrt(second_moment / (1.0 - jnp.power(BETA_TWO, step_count))) + ADAM_EPS)
        distance = jnp.left_shift(jnp.int32(1), ((step_index[0] + section) % levels).astype(jnp.int32))
        params = 0.5 * (params + jnp.roll(params, distance, axis=0)) - RATE * update
        mass = 0.5 * (mass + jnp.roll(mass, distance, axis=0))
    return (params, first_moment, second_moment, mass)
```

```python
import functools

import jax
import jax.numpy as jnp
from jax import lax
from jax.experimental import pallas as pl
from jax.experimental.pallas import tpu as pltpu
from jax.sharding import PartitionSpec as P

D = 7168
HEAD = 112
STEPS = 2
TOK = 256
NY = 4
NZ = 4
QUARTER = D // NY
SHARD_ROWS = QUARTER // NZ
LANES = 128
FLAT = SHARD_ROWS * HEAD // LANES
WIRE = FLAT + 8
GROUPS = SHARD_ROWS // 8
BLOCK = QUARTER + LANES

BETA_ONE = 0.9
BETA_TWO = 0.95
ADAM_EPS = 1e-08
RATE = 0.01

F32 = jnp.float32
BF16 = jnp.bfloat16
VMEM = pl.BlockSpec(memory_space=pltpu.VMEM)
SMEM = pl.BlockSpec(memory_space=pltpu.SMEM)
PARAMS = pltpu.CompilerParams(vmem_limit_bytes=40 * 1024 * 1024)

Z_GROUPS = [[y * NZ + z for z in range(NZ)] for y in range(NY)]
Y_GROUPS = [[y * NZ + z for y in range(NY)] for z in range(NZ)]


def shape(dims, dtype):
    return jax.ShapeDtypeStruct(dims, dtype)


def y_shift(array, by):
    pairs = [(y * NZ + z, (y + by) % NY * NZ + z) for y in range(NY) for z in range(NZ)]
    return lax.ppermute(array, "fsdp", pairs)


def gossip(array, distance):
    count = lax.axis_size("rep")
    return lax.ppermute(array, "rep", [(i, (i + distance) % count) for i in range(count)])


def lanes_of(rows):
    return lax.broadcasted_iota(jnp.int32, (rows, LANES), 1)


def flat_to_rows(flat, base, rows):
    lane = lanes_of(GROUPS)
    for j in range(8):
        if j == 0:
            part = flat[pl.ds(base, GROUPS, stride=7), :]
        else:
            part = flat[pl.ds(base + j - 1, GROUPS, stride=7), :]
            if j < 7:
                after = flat[pl.ds(base + j, GROUPS, stride=7), :]
                part = jnp.where(lane < LANES - 16 * j, after, part)
            part = pltpu.roll(part, 16 * j, 1)
        rows[pl.ds(j, GROUPS, stride=8), :] = jnp.where(lane < HEAD, part, 0.0)


def rows_to_flat(rows, base, flat):
    lane = lanes_of(GROUPS)
    for i in range(7):
        first = rows[pl.ds(base + i, GROUPS, stride=8), :]
        second = rows[pl.ds(base + i + 1, GROUPS, stride=8), :]
        if i:
            first = pltpu.roll(first, LANES - 16 * i, 1)
        second = pltpu.roll(second, HEAD - 16 * i, 1)
        flat[pl.ds(i, GROUPS, stride=7), :] = jnp.where(lane < HEAD - 16 * i, first, second)


def norm_kernel(place, tokens, cotangent, *outs):
    values = tokens[...].astype(F32)
    center = jnp.mean(values, axis=-1, keepdims=True)
    spread = jnp.mean((values - center) ** 2, axis=-1, keepdims=True)
    scale = lax.rsqrt(spread + 1e-05)
    cot = jnp.concatenate(
        [cotangent[...], jnp.zeros((cotangent.shape[0], LANES - HEAD), BF16)], axis=1
    )
    for k, out in enumerate(outs):
        start = pl.multiple_of((place[0] + k) % NY * QUARTER, LANES)
        part = tokens[:, pl.ds(start, QUARTER)].astype(F32)
        out[:, :QUARTER] = ((part - center) * scale).astype(BF16)
        out[:, QUARTER:] = cot


def norm(place, tokens, cotangent):
    rows = 64
    return pl.pallas_call(
        norm_kernel,
        grid=(TOK // rows,),
        in_specs=[
            SMEM,
            pl.BlockSpec((rows, D), lambda i: (i, 0)),
            pl.BlockSpec((rows, HEAD), lambda i: (i, 0)),
        ],
        out_specs=[pl.BlockSpec((rows, BLOCK), lambda i: (i, 0))] * NY,
        out_shape=[shape((TOK, BLOCK), BF16)] * NY,
        compiler_params=PARAMS,
        name="norm",
    )(place, tokens, cotangent)


def start_kernel(mass, params, own, wire):
    own[:FLAT, :] = params[...]
    own[FLAT:, :] = jnp.full((WIRE - FLAT, LANES), mass[0], F32)
    wire[...] = (own[...] / mass[0]).astype(BF16)


def start(mass, params):
    return pl.pallas_call(
        start_kernel,
        in_specs=[SMEM, VMEM],
        out_specs=[VMEM] * 2,
        out_shape=[shape((WIRE, LANES), F32), shape((WIRE, LANES), BF16)],
        compiler_params=PARAMS,
        name="start",
    )(mass, params)


def preact_kernel(place, wires, *refs):
    blocks, (out, flat, rows, weights) = refs[:NY], refs[NY:]
    flat[...] = wires[...].astype(F32)
    for s in range(NZ):
        flat_to_rows(flat, s * WIRE, rows)
        weights[pl.ds(s * SHARD_ROWS, SHARD_ROWS), :] = rows[...].astype(BF16)
    for k, block in enumerate(blocks):
        product = jnp.dot(block[:, :QUARTER], weights[...], preferred_element_type=F32)
        start = pl.multiple_of((place[0] + NY - k) % NY * TOK, TOK)
        out[pl.ds(start, TOK), :] = product[:, :HEAD].astype(BF16)


def partial_preact(place, wires, blocks):
    return pl.pallas_call(
        preact_kernel,
        in_specs=[SMEM] + [VMEM] * (1 + NY),
        out_specs=VMEM,
        out_shape=shape((NY * TOK, HEAD), BF16),
        scratch_shapes=[
            pltpu.VMEM((NZ * WIRE, LANES), F32),
            pltpu.VMEM((SHARD_ROWS, LANES), F32),
            pltpu.VMEM((QUARTER, LANES), BF16),
        ],
        compiler_params=PARAMS,
        name="partial_preact",
    )(place, wires, *blocks)


def grad_kernel(place, partials, *refs):
    blocks, (out, heads, rows, flat) = refs[:NY], refs[NY:]
    heads[...] = jnp.zeros_like(heads)
    total = jnp.zeros((LANES, QUARTER), F32)
    for k, block in enumerate(blocks):
        start = pl.multiple_of((place[0] + NY - k) % NY * TOK, TOK)
        preact = jnp.zeros((TOK, HEAD), F32)
        for s in range(NY):
            preact = preact + partials[pl.ds(s * NY * TOK + start, TOK), :].astype(F32)
        cot = block[:, QUARTER:QUARTER + HEAD].astype(F32)
        sig = 1.0 / (1.0 + jnp.exp(-preact))
        heads[:, :HEAD] = (cot * sig * (1.0 + preact * (1.0 - sig))).astype(BF16)
        total = total + lax.dot_general(
            heads[...], block[:, :QUARTER], (((0,), (0,)), ((), ())), preferred_element_type=F32
        )
    rows[...] = total.T
    flat[FLAT:, :] = jnp.zeros((WIRE - FLAT, LANES), F32)
    for s in range(NZ):
        rows_to_flat(rows, s * SHARD_ROWS, flat)
        out[s] = flat[...].astype(BF16)


def quarter_grad(place, partials, blocks):
    return pl.pallas_call(
        grad_kernel,
        in_specs=[SMEM] + [VMEM] * (1 + NY),
        out_specs=VMEM,
        out_shape=shape((NZ, WIRE, LANES), BF16),
        scratch_shapes=[
            pltpu.VMEM((TOK, LANES), BF16),
            pltpu.VMEM((QUARTER, LANES), F32),
            pltpu.VMEM((WIRE, LANES), F32),
        ],
        compiler_params=PARAMS,
        name="quarter_grad",
    )(place, partials, *blocks)


def adam(section, scales, terms, first_moment, second_moment, own, peer):
    grads = terms[0].astype(F32)
    for s in range(1, NZ):
        grads = grads + terms[s].astype(F32)
    grads = grads[:FLAT, :]
    first = BETA_ONE * first_moment[...] + (1.0 - BETA_ONE) * grads
    second = BETA_TWO * second_moment[...] + (1.0 - BETA_TWO) * grads * grads
    update = first / scales[2 * section] / (jnp.sqrt(second / scales[2 * section + 1]) + ADAM_EPS)
    mixed = 0.5 * (own[...] + peer[...])
    return first, second, mixed[:FLAT, :] - RATE * update, mixed[FLAT:, :]


def between_kernel(scales, terms, first_moment, second_moment, own, peer, *outs):
    new_first, new_second, new_own, wire = outs
    first, second, params, mass = adam(
        0, scales, terms, first_moment, second_moment, own, peer
    )
    new_first[...] = first
    new_second[...] = second
    new_own[:FLAT, :] = params
    new_own[FLAT:, :] = mass
    wire[...] = (new_own[...] / mass[0:1, :]).astype(BF16)


def between(scales, terms, first_moment, second_moment, own, peer):
    return pl.pallas_call(
        between_kernel,
        in_specs=[SMEM] + [VMEM] * 5,
        out_specs=[VMEM] * 4,
        out_shape=[
            shape((FLAT, LANES), F32),
            shape((FLAT, LANES), F32),
            shape((WIRE, LANES), F32),
            shape((WIRE, LANES), BF16),
        ],
        compiler_params=PARAMS,
        name="between",
    )(scales, terms, first_moment, second_moment, own, peer)


def last_kernel(scales, terms, first_moment, second_moment, own, peer, *outs):
    new_params, new_first, new_second, new_mass = outs
    first, second, params, mass = adam(
        1, scales, terms, first_moment, second_moment, own, peer
    )
    new_first[...] = first
    new_second[...] = second
    new_params[...] = params
    new_mass[0] = mass[0, 0]


def last(scales, terms, first_moment, second_moment, own, peer):
    return pl.pallas_call(
        last_kernel,
        in_specs=[SMEM] + [VMEM] * 5,
        out_specs=[VMEM] * 3 + [SMEM],
        out_shape=[shape((FLAT, LANES), F32)] * 3 + [shape((1,), F32)],
        compiler_params=PARAMS,
        name="last",
    )(scales, terms, first_moment, second_moment, own, peer)


def steps_at(level, levels, tokens, cotangent, params, first_moment, second_moment, mass, scales):
    place = (lax.axis_index("fsdp") // NZ).astype(jnp.int32).reshape(1)
    own, wire = start(mass, params)
    blocks = norm(place, tokens, cotangent)
    blocks = [blocks[0]] + [y_shift(blocks[k], k) for k in range(1, NY)]
    for section in range(STEPS):
        peer = gossip(own, 2 ** ((level + section) % levels))
        wires = lax.all_gather(wire, "fsdp", axis=0, tiled=True, axis_index_groups=Z_GROUPS)
        partial = partial_preact(place, wires, blocks)
        partials = lax.all_gather(partial, "fsdp", axis=0, tiled=True, axis_index_groups=Y_GROUPS)
        terms = quarter_grad(place, partials, blocks)
        terms = lax.all_to_all(terms, "fsdp", 0, 0, axis_index_groups=Z_GROUPS)
        if section < STEPS - 1:
            first_moment, second_moment, own, wire = between(
                scales, terms, first_moment, second_moment, own, peer
            )
    return last(scales, terms, first_moment, second_moment, own, peer)


def on_device(tokens, cotangent, params, first_moment, second_moment, mass, step_index):
    levels = lax.axis_size("rep").bit_length() - 1
    counts = (step_index[0] + 1 + jnp.arange(STEPS)).astype(F32)
    scales = jnp.stack(
        [1.0 - jnp.power(BETA_ONE, counts), 1.0 - jnp.power(BETA_TWO, counts)], axis=1
    ).reshape(-1)
    flat = [array.reshape(FLAT, LANES) for array in (params, first_moment, second_moment)]
    new_params, new_first, new_second, new_mass = lax.switch(
        step_index[0] % levels,
        [functools.partial(steps_at, level, levels) for level in range(levels)],
        tokens[0], cotangent[0], *flat, mass, scales,
    )
    return tuple(array.reshape(1, -1) for array in (new_params, new_first, new_second)) + (new_mass,)


def solution(mesh):
    placed = (
        P("rep", "fsdp", None),
        P("rep", "fsdp", None),
        P("rep", "fsdp"),
        P("rep", "fsdp"),
        P("rep", "fsdp"),
        P("rep"),
        P(),
    )
    return jax.shard_map(
        on_device,
        mesh=mesh,
        in_specs=placed,
        out_specs=(P("rep", "fsdp"), P("rep", "fsdp"), P("rep", "fsdp"), P("rep")),
        check_vma=False,
    )
```

```python
import functools

import jax
import jax.numpy as jnp
from jax import lax
from jax.experimental import pallas as pl
from jax.experimental.pallas import tpu as pltpu
from jax.sharding import PartitionSpec as P

D = 7168
HEAD = 112
STEPS = 2
TOK = 256
NY = 4
NZ = 4
QUARTER = D // NY
SHARD_ROWS = QUARTER // NZ
LANES = 128
FLAT = SHARD_ROWS * HEAD // LANES
WIRE = FLAT + 8
GROUPS = SHARD_ROWS // 8
BLOCK = QUARTER + LANES

BETA_ONE = 0.9
BETA_TWO = 0.95
ADAM_EPS = 1e-08
RATE = 0.01

F32 = jnp.float32
BF16 = jnp.bfloat16
VMEM = pl.BlockSpec(memory_space=pltpu.VMEM)
SMEM = pl.BlockSpec(memory_space=pltpu.SMEM)
PARAMS = pltpu.CompilerParams(vmem_limit_bytes=40 * 1024 * 1024)

Z_GROUPS = [[y * NZ + z for z in range(NZ)] for y in range(NY)]
Y_GROUPS = [[y * NZ + z for y in range(NY)] for z in range(NZ)]


def shape(dims, dtype):
    return jax.ShapeDtypeStruct(dims, dtype)


def y_shift(array, by):
    pairs = [(y * NZ + z, (y + by) % NY * NZ + z) for y in range(NY) for z in range(NZ)]
    return lax.ppermute(array, "fsdp", pairs)


def gossip(array, distance):
    count = lax.axis_size("rep")
    return lax.ppermute(array, "rep", [(i, (i + distance) % count) for i in range(count)])


def lanes_of(rows):
    return lax.broadcasted_iota(jnp.int32, (rows, LANES), 1)


def flat_to_rows(flat, base, rows):
    lane = lanes_of(GROUPS)
    for j in range(8):
        if j == 0:
            part = flat[pl.ds(base, GROUPS, stride=7), :]
        else:
            part = flat[pl.ds(base + j - 1, GROUPS, stride=7), :]
            if j < 7:
                after = flat[pl.ds(base + j, GROUPS, stride=7), :]
                part = jnp.where(lane < LANES - 16 * j, after, part)
            part = pltpu.roll(part, 16 * j, 1)
        rows[pl.ds(j, GROUPS, stride=8), :] = jnp.where(lane < HEAD, part, 0.0)


def rows_to_flat(rows, base, flat):
    lane = lanes_of(GROUPS)
    for i in range(7):
        first = rows[pl.ds(base + i, GROUPS, stride=8), :]
        second = rows[pl.ds(base + i + 1, GROUPS, stride=8), :]
        if i:
            first = pltpu.roll(first, LANES - 16 * i, 1)
        second = pltpu.roll(second, HEAD - 16 * i, 1)
        flat[pl.ds(i, GROUPS, stride=7), :] = jnp.where(lane < HEAD - 16 * i, first, second)


def norm_kernel(place, tokens, cotangent, *outs):
    values = tokens[...].astype(F32)
    center = jnp.mean(values, axis=-1, keepdims=True)
    spread = jnp.mean((values - center) ** 2, axis=-1, keepdims=True)
    scale = lax.rsqrt(spread + 1e-05)
    cot = jnp.concatenate(
        [cotangent[...], jnp.zeros((LANES - HEAD, cotangent.shape[1]), BF16)], axis=0
    ).T
    for k, out in enumerate(outs):
        start = pl.multiple_of((place[0] + k) % NY * QUARTER, LANES)
        part = tokens[:, pl.ds(start, QUARTER)].astype(F32)
        out[:, :QUARTER] = ((part - center) * scale).astype(BF16)
        out[:, QUARTER:] = cot


def norm(place, tokens, cotangent):
    rows = 128
    return pl.pallas_call(
        norm_kernel,
        grid=(TOK // rows,),
        in_specs=[
            SMEM,
            pl.BlockSpec((rows, D), lambda i: (i, 0)),
            pl.BlockSpec((HEAD, rows), lambda i: (0, i)),
        ],
        out_specs=[pl.BlockSpec((rows, BLOCK), lambda i: (i, 0))] * NY,
        out_shape=[shape((TOK, BLOCK), BF16)] * NY,
        compiler_params=PARAMS,
        name="norm",
    )(place, tokens, cotangent)


def start_kernel(mass, params, own, wire):
    own[:FLAT, :] = params[...]
    own[FLAT:, :] = jnp.full((WIRE - FLAT, LANES), mass[0], F32)
    wire[...] = (own[...] / mass[0]).astype(BF16)


def start(mass, params):
    return pl.pallas_call(
        start_kernel,
        in_specs=[SMEM, VMEM],
        out_specs=[VMEM] * 2,
        out_shape=[shape((WIRE, LANES), F32), shape((WIRE, LANES), BF16)],
        compiler_params=PARAMS,
        name="start",
    )(mass, params)


def preact_kernel(place, wires, *refs):
    blocks, (out, flat, rows, weights) = refs[:NY], refs[NY:]
    flat[...] = wires[...].astype(F32)
    for s in range(NZ):
        flat_to_rows(flat, s * WIRE, rows)
        weights[pl.ds(s * SHARD_ROWS, SHARD_ROWS), :] = rows[...].astype(BF16)
    for k, block in enumerate(blocks):
        product = jnp.dot(block[:, :QUARTER], weights[...], preferred_element_type=F32)
        start = pl.multiple_of((place[0] + NY - k) % NY * TOK, TOK)
        out[pl.ds(start, TOK), :] = product[:, :HEAD].astype(BF16)


def partial_preact(place, wires, blocks):
    return pl.pallas_call(
        preact_kernel,
        in_specs=[SMEM] + [VMEM] * (1 + NY),
        out_specs=VMEM,
        out_shape=shape((NY * TOK, HEAD), BF16),
        scratch_shapes=[
            pltpu.VMEM((NZ * WIRE, LANES), F32),
            pltpu.VMEM((SHARD_ROWS, LANES), F32),
            pltpu.VMEM((QUARTER, LANES), BF16),
        ],
        compiler_params=PARAMS,
        name="partial_preact",
    )(place, wires, *blocks)


def grad_kernel(place, partials, *refs):
    blocks, (out, heads, rows, flat) = refs[:NY], refs[NY:]
    heads[...] = jnp.zeros_like(heads)
    total = jnp.zeros((LANES, QUARTER), F32)
    for k, block in enumerate(blocks):
        start = pl.multiple_of((place[0] + NY - k) % NY * TOK, TOK)
        preact = jnp.zeros((TOK, HEAD), F32)
        for s in range(NY):
            preact = preact + partials[pl.ds(s * NY * TOK + start, TOK), :].astype(F32)
        cot = block[:, QUARTER:QUARTER + HEAD].astype(F32)
        sig = 1.0 / (1.0 + jnp.exp(-preact))
        heads[:, :HEAD] = (cot * sig * (1.0 + preact * (1.0 - sig))).astype(BF16)
        total = total + lax.dot_general(
            heads[...], block[:, :QUARTER], (((0,), (0,)), ((), ())), preferred_element_type=F32
        )
    rows[...] = total.T
    flat[FLAT:, :] = jnp.zeros((WIRE - FLAT, LANES), F32)
    for s in range(NZ):
        rows_to_flat(rows, s * SHARD_ROWS, flat)
        out[s] = flat[...].astype(BF16)


def quarter_grad(place, partials, blocks):
    return pl.pallas_call(
        grad_kernel,
        in_specs=[SMEM] + [VMEM] * (1 + NY),
        out_specs=VMEM,
        out_shape=shape((NZ, WIRE, LANES), BF16),
        scratch_shapes=[
            pltpu.VMEM((TOK, LANES), BF16),
            pltpu.VMEM((QUARTER, LANES), F32),
            pltpu.VMEM((WIRE, LANES), F32),
        ],
        compiler_params=PARAMS,
        name="quarter_grad",
    )(place, partials, *blocks)


def adam(section, scales, terms, first_moment, second_moment, own, peer):
    grads = terms[0].astype(F32)
    for s in range(1, NZ):
        grads = grads + terms[s].astype(F32)
    grads = grads[:FLAT, :]
    first = BETA_ONE * first_moment[...] + (1.0 - BETA_ONE) * grads
    second = BETA_TWO * second_moment[...] + (1.0 - BETA_TWO) * grads * grads
    update = first / scales[2 * section] / (jnp.sqrt(second / scales[2 * section + 1]) + ADAM_EPS)
    mixed = 0.5 * (own[...] + peer[...])
    return first, second, mixed[:FLAT, :] - RATE * update, mixed[FLAT:, :]


def between_kernel(scales, terms, first_moment, second_moment, own, peer, *outs):
    new_first, new_second, new_own, wire = outs
    first, second, params, mass = adam(
        0, scales, terms, first_moment, second_moment, own, peer
    )
    new_first[...] = first
    new_second[...] = second
    new_own[:FLAT, :] = params
    new_own[FLAT:, :] = mass
    wire[...] = (new_own[...] / mass[0:1, :]).astype(BF16)


def between(scales, terms, first_moment, second_moment, own, peer):
    return pl.pallas_call(
        between_kernel,
        in_specs=[SMEM] + [VMEM] * 5,
        out_specs=[VMEM] * 4,
        out_shape=[
            shape((FLAT, LANES), F32),
            shape((FLAT, LANES), F32),
            shape((WIRE, LANES), F32),
            shape((WIRE, LANES), BF16),
        ],
        compiler_params=PARAMS,
        name="between",
    )(scales, terms, first_moment, second_moment, own, peer)


def last_kernel(scales, terms, first_moment, second_moment, own, peer, *outs):
    new_params, new_first, new_second, new_mass = outs
    first, second, params, mass = adam(
        1, scales, terms, first_moment, second_moment, own, peer
    )
    new_first[...] = first
    new_second[...] = second
    new_params[...] = params
    new_mass[0] = mass[0, 0]


def last(scales, terms, first_moment, second_moment, own, peer):
    return pl.pallas_call(
        last_kernel,
        in_specs=[SMEM] + [VMEM] * 5,
        out_specs=[VMEM] * 3 + [SMEM],
        out_shape=[shape((FLAT, LANES), F32)] * 3 + [shape((1,), F32)],
        compiler_params=PARAMS,
        name="last",
    )(scales, terms, first_moment, second_moment, own, peer)


def exchange(distance, partial, own):
    peer = gossip(own, distance)
    partials = lax.all_gather(partial, "fsdp", axis=0, tiled=True, axis_index_groups=Y_GROUPS)
    return partials, peer


def on_device(tokens, cotangent, params, first_moment, second_moment, mass, step_index):
    levels = lax.axis_size("rep").bit_length() - 1
    counts = (step_index[0] + 1 + jnp.arange(STEPS)).astype(F32)
    scales = jnp.stack(
        [1.0 - jnp.power(BETA_ONE, counts), 1.0 - jnp.power(BETA_TWO, counts)], axis=1
    ).reshape(-1)
    place = (lax.axis_index("fsdp") // NZ).astype(jnp.int32).reshape(1)
    first_moment = first_moment.reshape(FLAT, LANES)
    second_moment = second_moment.reshape(FLAT, LANES)
    own, wire = start(mass, params.reshape(FLAT, LANES))
    picks = [(step_index[0] + section) % levels for section in range(STEPS)]
    wire, scales, *picks = lax.optimization_barrier((wire, scales, *picks))
    blocks = norm(place, tokens[0], cotangent[0].T)
    blocks = [blocks[0]] + [y_shift(blocks[k], k) for k in range(1, NY)]
    for section in range(STEPS):
        wires = lax.all_gather(wire, "fsdp", axis=0, tiled=True, axis_index_groups=Z_GROUPS)
        partial = partial_preact(place, wires, blocks)
        partials, peer = lax.switch(
            picks[section],
            [functools.partial(exchange, 2**level) for level in range(levels)],
            partial, own,
        )
        terms = quarter_grad(place, partials, blocks)
        terms = lax.all_to_all(terms, "fsdp", 0, 0, axis_index_groups=Z_GROUPS)
        if section < STEPS - 1:
            first_moment, second_moment, own, wire = between(
                scales, terms, first_moment, second_moment, own, peer
            )
    *new, new_mass = last(scales, terms, first_moment, second_moment, own, peer)
    return tuple(array.reshape(1, -1) for array in new) + (new_mass,)


def solution(mesh):
    placed = (
        P("rep", "fsdp", None),
        P("rep", "fsdp", None),
        P("rep", "fsdp"),
        P("rep", "fsdp"),
        P("rep", "fsdp"),
        P("rep"),
        P(),
    )
    return jax.shard_map(
        on_device,
        mesh=mesh,
        in_specs=placed,
        out_specs=(P("rep", "fsdp"), P("rep", "fsdp"), P("rep", "fsdp"), P("rep")),
        check_vma=False,
    )
```

```python
import functools

import jax
import jax.numpy as jnp
from jax import lax
from jax.experimental import pallas as pl
from jax.experimental.pallas import tpu as pltpu
from jax.sharding import PartitionSpec as P

D = 7168
HEAD = 112
STEPS = 2
TOK = 256
NY = 4
NZ = 4
QUARTER = D // NY
SHARD_ROWS = QUARTER // NZ
LANES = 128
FLAT = SHARD_ROWS * HEAD // LANES
WIRE = FLAT + 8
GROUPS = SHARD_ROWS // 8
BLOCK = QUARTER + LANES
CHUNKS = 4
CHUNK = TOK // CHUNKS

BETA_ONE = 0.9
BETA_TWO = 0.95
ADAM_EPS = 1e-08
RATE = 0.01

F32 = jnp.float32
BF16 = jnp.bfloat16
VMEM = pl.BlockSpec(memory_space=pltpu.VMEM)
SMEM = pl.BlockSpec(memory_space=pltpu.SMEM)
HBM = pl.BlockSpec(memory_space=pltpu.HBM)
DMA = pltpu.SemaphoreType.DMA
PARAMS = pltpu.CompilerParams(vmem_limit_bytes=40 * 1024 * 1024)

Z_GROUPS = [[y * NZ + z for z in range(NZ)] for y in range(NY)]
Y_GROUPS = [[y * NZ + z for y in range(NY)] for z in range(NZ)]


def in_hbm(array):
    return pltpu.with_memory_space_constraint(array, pltpu.HBM)


def shape(dims, dtype):
    return jax.ShapeDtypeStruct(dims, dtype)


def y_shift(array, by):
    pairs = [(y * NZ + z, (y + by) % NY * NZ + z) for y in range(NY) for z in range(NZ)]
    return lax.ppermute(array, "fsdp", pairs)


def gossip(array, distance):
    count = lax.axis_size("rep")
    return lax.ppermute(array, "rep", [(i, (i + distance) % count) for i in range(count)])


def lanes_of(rows):
    return lax.broadcasted_iota(jnp.int32, (rows, LANES), 1)


def flat_to_rows(flat, base, rows):
    lane = lanes_of(GROUPS)
    for j in range(8):
        if j == 0:
            part = flat[pl.ds(base, GROUPS, stride=7), :]
        else:
            part = flat[pl.ds(base + j - 1, GROUPS, stride=7), :]
            if j < 7:
                after = flat[pl.ds(base + j, GROUPS, stride=7), :]
                part = jnp.where(lane < LANES - 16 * j, after, part)
            part = pltpu.roll(part, 16 * j, 1)
        rows[pl.ds(j, GROUPS, stride=8), :] = jnp.where(lane < HEAD, part, 0.0)


def rows_to_flat(rows, base, flat):
    lane = lanes_of(GROUPS)
    for i in range(7):
        first = rows[pl.ds(base + i, GROUPS, stride=8), :]
        second = rows[pl.ds(base + i + 1, GROUPS, stride=8), :]
        if i:
            first = pltpu.roll(first, LANES - 16 * i, 1)
        second = pltpu.roll(second, HEAD - 16 * i, 1)
        flat[pl.ds(i, GROUPS, stride=7), :] = jnp.where(lane < HEAD - 16 * i, first, second)


def norm_kernel(place, tokens, cotangent, *refs):
    (own, *far), (values, cot, near, sems, out_sems) = refs[:NY], refs[NY:]
    chunks = [pl.ds(i * CHUNK, CHUNK) for i in range(CHUNKS)]
    copies = [
        pltpu.make_async_copy(tokens.at[rows], values.at[rows], sems.at[i])
        for i, rows in enumerate(chunks)
    ]
    copies.append(pltpu.make_async_copy(cotangent, cot, sems.at[CHUNKS]))
    for copy in (copies[-1], *copies[:-1]):
        copy.start()
    outs = [own, *(near.at[k] for k in range(NY - 1))]
    copies[-1].wait()
    padded = jnp.concatenate([cot[...], jnp.zeros((LANES - HEAD, TOK), BF16)], axis=0).T
    for out in outs:
        out[:, QUARTER:] = padded
    sent = []
    for i, rows in enumerate(chunks):
        copies[i].wait()
        totals = [jnp.zeros((CHUNK, LANES), F32) for _ in range(4)]
        for c in range(D // LANES):
            totals[c % 4] += values[rows, c * LANES:(c + 1) * LANES].astype(F32)
        center = jnp.sum(sum(totals), axis=-1, keepdims=True) * (1.0 / D)
        center = jnp.broadcast_to(center, (CHUNK, LANES))
        totals = [jnp.zeros((CHUNK, LANES), F32) for _ in range(2)]
        for c in range(D // LANES):
            apart = values[rows, c * LANES:(c + 1) * LANES].astype(F32) - center
            totals[c % 2] += apart * apart
        spread = jnp.sum(sum(totals), axis=-1, keepdims=True) * (1.0 / D)
        scale = jnp.broadcast_to(lax.rsqrt(spread + 1e-05), (CHUNK, LANES))
        for k in (*range(1, NY), 0):
            start = (place[0] + k) % NY * QUARTER
            for c in range(QUARTER // LANES):
                lanes = pl.ds(pl.multiple_of(start + c * LANES, LANES), LANES)
                part = (values[rows, lanes].astype(F32) - center) * scale
                outs[k][rows, c * LANES:(c + 1) * LANES] = part.astype(BF16)
            if k:
                sent.append(
                    pltpu.make_async_copy(
                        near.at[k - 1, rows], far[k - 1].at[rows], out_sems.at[i, k - 1]
                    )
                )
                sent[-1].start()
    for copy in sent:
        copy.wait()


def norm(place, tokens, cotangent):
    return pl.pallas_call(
        norm_kernel,
        in_specs=[SMEM, HBM, HBM],
        out_specs=[VMEM] + [HBM] * (NY - 1),
        out_shape=[shape((TOK, BLOCK), BF16)] + [pltpu.HBM((TOK, BLOCK), BF16)] * (NY - 1),
        scratch_shapes=[
            pltpu.VMEM((TOK, D), BF16),
            pltpu.VMEM((HEAD, TOK), BF16),
            pltpu.VMEM((NY - 1, TOK, BLOCK), BF16),
            DMA((CHUNKS + 1,)),
            DMA((CHUNKS, NY - 1)),
        ],
        compiler_params=PARAMS,
        name="norm",
    )(place, in_hbm(tokens), in_hbm(cotangent))


def start_kernel(mass, params, own, wire):
    own[:FLAT, :] = params[...]
    own[FLAT:, :] = jnp.full((WIRE - FLAT, LANES), mass[0], F32)
    wire[...] = (own[...] / mass[0]).astype(BF16)


def start(mass, params):
    return pl.pallas_call(
        start_kernel,
        in_specs=[SMEM, VMEM],
        out_specs=[VMEM] * 2,
        out_shape=[shape((WIRE, LANES), F32), shape((WIRE, LANES), BF16)],
        compiler_params=PARAMS,
        name="start",
    )(mass, params)


def preact_kernel(place, wires, *refs):
    blocks, (out, flat, rows, weights, held, sem) = refs[:NY], refs[NY:]
    fetch = pltpu.make_async_copy(blocks[-1], held, sem)
    fetch.start()
    flat[...] = wires[...].astype(F32)
    for s in range(NZ):
        flat_to_rows(flat, s * WIRE, rows)
        weights[pl.ds(s * SHARD_ROWS, SHARD_ROWS), :] = rows[...].astype(BF16)
    for k, block in enumerate((*blocks[:-1], held)):
        if block is held:
            fetch.wait()
        product = jnp.dot(block[:, :QUARTER], weights[...], preferred_element_type=F32)
        start = pl.multiple_of((place[0] + NY - k) % NY * TOK, TOK)
        out[pl.ds(start, TOK), :] = product[:, :HEAD].astype(BF16)


def partial_preact(place, wires, blocks):
    return pl.pallas_call(
        preact_kernel,
        in_specs=[SMEM] + [VMEM] * NY + [HBM],
        out_specs=VMEM,
        out_shape=shape((NY * TOK, HEAD), BF16),
        scratch_shapes=[
            pltpu.VMEM((NZ * WIRE, LANES), F32),
            pltpu.VMEM((SHARD_ROWS, LANES), F32),
            pltpu.VMEM((QUARTER, LANES), BF16),
            pltpu.VMEM((TOK, BLOCK), BF16),
            DMA,
        ],
        compiler_params=PARAMS,
        name="partial_preact",
    )(place, wires, *blocks[:-1], in_hbm(blocks[-1]))


def grad_kernel(near, place, partials, *refs):
    blocks, refs = refs[:NY], refs[NY:]
    if near:
        states, (out, near_first, near_second, mixed), refs = refs[:4], refs[4:8], refs[8:]
        heads, rows, flat, held, near_peer, sems = refs
        pairs = [(blocks[-1], held), *zip(states, (near_first, near_second, mixed, near_peer))]
    else:
        out, heads, rows, flat, held, sems = refs
        pairs = [(blocks[-1], held)]
    copies = [
        pltpu.make_async_copy(source, into, sems.at[i]) for i, (source, into) in enumerate(pairs)
    ]
    for copy in copies:
        copy.start()
    heads[...] = jnp.zeros_like(heads)
    total = jnp.zeros((LANES, QUARTER), F32)
    for k, block in enumerate((*blocks[:-1], held)):
        start = pl.multiple_of((place[0] + NY - k) % NY * TOK, TOK)
        preact = jnp.zeros((TOK, HEAD), F32)
        for s in range(NY):
            preact = preact + partials[pl.ds(s * NY * TOK + start, TOK), :].astype(F32)
        if block is held:
            copies[0].wait()
        cot = block[:, QUARTER:QUARTER + HEAD].astype(F32)
        sig = 1.0 / (1.0 + jnp.exp(-preact))
        heads[:, :HEAD] = (cot * sig * (1.0 + preact * (1.0 - sig))).astype(BF16)
        total = total + lax.dot_general(
            heads[...], block[:, :QUARTER], (((0,), (0,)), ((), ())), preferred_element_type=F32
        )
    rows[...] = total.T
    flat[FLAT:, :] = jnp.zeros((WIRE - FLAT, LANES), F32)
    for s in range(NZ):
        rows_to_flat(rows, s * SHARD_ROWS, flat)
        out[s] = flat[...].astype(BF16)
    if near:
        for copy in copies[1:]:
            copy.wait()
        mixed[...] = 0.5 * (mixed[...] + near_peer[...])


def quarter_grad(place, partials, blocks, *states):
    near = bool(states)
    return pl.pallas_call(
        functools.partial(grad_kernel, near),
        in_specs=[SMEM] + [VMEM] * NY + [HBM] * (1 + len(states)),
        out_specs=[VMEM] * (4 if near else 1),
        out_shape=[
            shape((NZ, WIRE, LANES), BF16),
            shape((FLAT, LANES), F32),
            shape((FLAT, LANES), F32),
            shape((WIRE, LANES), F32),
        ][:4 if near else 1],
        scratch_shapes=[
            pltpu.VMEM((TOK, LANES), BF16),
            pltpu.VMEM((QUARTER, LANES), F32),
            pltpu.VMEM((WIRE, LANES), F32),
            pltpu.VMEM((TOK, BLOCK), BF16),
            *[pltpu.VMEM((WIRE, LANES), F32)] * near,
            DMA((1 + len(states),)),
        ],
        compiler_params=PARAMS,
        name="quarter_grad",
    )(place, partials, *blocks[:-1], in_hbm(blocks[-1]), *map(in_hbm, states))


def adam(section, scales, terms, first_moment, second_moment, mixed):
    grads = terms[0].astype(F32)
    for s in range(1, NZ):
        grads = grads + terms[s].astype(F32)
    grads = grads[:FLAT, :]
    first = BETA_ONE * first_moment[...] + (1.0 - BETA_ONE) * grads
    second = BETA_TWO * second_moment[...] + (1.0 - BETA_TWO) * grads * grads
    update = first / scales[2 * section] / (jnp.sqrt(second / scales[2 * section + 1]) + ADAM_EPS)
    return first, second, mixed[:FLAT, :] - RATE * update, mixed[FLAT:, :]


def between_kernel(scales, terms, *refs):
    states, (far_first, far_second, new_own, wire), refs = refs[:4], refs[4:8], refs[8:]
    first_moment, second_moment, own, peer, new_first, new_second, sems = refs
    pairs = [
        *zip(states, (first_moment, second_moment, own, peer)),
        (new_first, far_first), (new_second, far_second),
    ]
    copies = [
        pltpu.make_async_copy(source, into, sems.at[i]) for i, (source, into) in enumerate(pairs)
    ]
    for copy in copies[:4]:
        copy.start()
    for copy in copies[:4]:
        copy.wait()
    own[...] = 0.5 * (own[...] + peer[...])
    first, second, params, mass = adam(0, scales, terms, first_moment, second_moment, own)
    new_first[...] = first
    new_second[...] = second
    for copy in copies[4:]:
        copy.start()
    new_own[:FLAT, :] = params
    new_own[FLAT:, :] = mass
    wire[...] = (new_own[...] / mass[0:1, :]).astype(BF16)
    for copy in copies[4:]:
        copy.wait()


def between(scales, terms, *states):
    flat, wide = pltpu.VMEM((FLAT, LANES), F32), pltpu.VMEM((WIRE, LANES), F32)
    return pl.pallas_call(
        between_kernel,
        in_specs=[SMEM, VMEM] + [HBM] * 4,
        out_specs=[HBM] * 2 + [VMEM] * 2,
        out_shape=[
            pltpu.HBM((FLAT, LANES), F32),
            pltpu.HBM((FLAT, LANES), F32),
            shape((WIRE, LANES), F32),
            shape((WIRE, LANES), BF16),
        ],
        scratch_shapes=[flat, flat, wide, wide, flat, flat, DMA((6,))],
        compiler_params=PARAMS,
        name="between",
    )(scales, terms, *map(in_hbm, states))


def last_kernel(scales, terms, first_moment, second_moment, mixed, *outs):
    new_params, new_first, new_second, new_mass = outs
    first, second, params, mass = adam(1, scales, terms, first_moment, second_moment, mixed)
    new_first[...] = first
    new_second[...] = second
    new_params[...] = params
    new_mass[0] = mass[0, 0]


def last(scales, *arrays):
    return pl.pallas_call(
        last_kernel,
        in_specs=[SMEM] + [VMEM] * 4,
        out_specs=[VMEM] * 3 + [SMEM],
        out_shape=[shape((FLAT, LANES), F32)] * 3 + [shape((1,), F32)],
        compiler_params=PARAMS,
        name="last",
    )(scales, *arrays)


def gather(array, groups):
    return lax.all_gather(array, "fsdp", axis=0, tiled=True, axis_index_groups=groups)


def gossip_alone(distance, own):
    return gossip(own, distance)


def gossip_beside(distance, own, wire):
    return gossip(own, distance), gather(wire, Z_GROUPS)


def at_level(pick, levels, function, *operands):
    return lax.switch(
        pick, [functools.partial(function, 2**level) for level in range(levels)], *operands
    )


def on_device(tokens, cotangent, params, first_moment, second_moment, mass, step_index):
    levels = lax.axis_size("rep").bit_length() - 1
    counts = (step_index[0] + 1 + jnp.arange(STEPS)).astype(F32)
    scales = jnp.stack(
        [1.0 - jnp.power(BETA_ONE, counts), 1.0 - jnp.power(BETA_TWO, counts)], axis=1
    ).reshape(-1)
    picks = [(step_index[0] + section) % levels for section in range(STEPS)]
    place = (lax.axis_index("fsdp") // NZ).astype(jnp.int32).reshape(1)
    first_moment = first_moment.reshape(FLAT, LANES)
    second_moment = second_moment.reshape(FLAT, LANES)
    own, wire = start(mass, params.reshape(FLAT, LANES))
    wire, scales, *picks = lax.optimization_barrier((wire, scales, *picks))
    blocks = norm(place, tokens[0], cotangent[0].T)
    blocks = [blocks[0]] + [y_shift(blocks[k], k) for k in range(1, NY)]
    for section in range(STEPS):
        if section == 0:
            wires = gather(wire, Z_GROUPS)
            wires, own = lax.optimization_barrier((wires, own))
            peer = at_level(picks[section], levels, gossip_alone, own)
            wires, peer = lax.optimization_barrier((wires, peer))
        else:
            peer, wires = at_level(picks[section], levels, gossip_beside, own, wire)
        partials = gather(partial_preact(place, wires, blocks), Y_GROUPS)
        states = first_moment, second_moment, own, peer
        terms, *near = quarter_grad(place, partials, blocks, *(states if section else ()))
        terms = lax.all_to_all(terms, "fsdp", 0, 0, axis_index_groups=Z_GROUPS)
        terms, *picks = lax.optimization_barrier((terms, *picks))
        if section < STEPS - 1:
            first_moment, second_moment, own, wire = between(scales, terms, *states)
    *new, new_mass = last(scales, terms, *near)
    return tuple(array.reshape(1, -1) for array in new) + (new_mass,)


def solution(mesh):
    placed = (
        P("rep", "fsdp", None),
        P("rep", "fsdp", None),
        P("rep", "fsdp"),
        P("rep", "fsdp"),
        P("rep", "fsdp"),
        P("rep"),
        P(),
    )
    return jax.shard_map(
        on_device,
        mesh=mesh,
        in_specs=placed,
        out_specs=(P("rep", "fsdp"), P("rep", "fsdp"), P("rep", "fsdp"), P("rep")),
        check_vma=False,
    )
```

```python
import functools

import jax
import jax.numpy as jnp
from jax import lax
from jax.experimental import pallas as pl
from jax.experimental.pallas import tpu as pltpu
from jax.sharding import PartitionSpec as P

D = 7168
HEAD = 112
STEPS = 2
TOK = 256
NY = 4
NZ = 4
QUARTER = D // NY
SHARD_ROWS = QUARTER // NZ
LANES = 128
FLAT = SHARD_ROWS * HEAD // LANES
WIRE = FLAT + 8
GROUPS = SHARD_ROWS // 8
BLOCK = QUARTER + LANES
CHUNKS = 4
CHUNK = TOK // CHUNKS
HALF = TOK // 2
EARLY = ((2, 0, HALF),)
LATER = ((2, HALF, HALF), (1, 0, TOK), (3, 0, TOK), (0, 0, TOK))
PARTS = (LATER[3], LATER[1], EARLY[0], LATER[0], LATER[2])

BETA_ONE = 0.9
BETA_TWO = 0.95
ADAM_EPS = 1e-08
RATE = 0.01

F32 = jnp.float32
BF16 = jnp.bfloat16
VMEM = pl.BlockSpec(memory_space=pltpu.VMEM)
SMEM = pl.BlockSpec(memory_space=pltpu.SMEM)
HBM = pl.BlockSpec(memory_space=pltpu.HBM)
DMA = pltpu.SemaphoreType.DMA
PARAMS = pltpu.CompilerParams(vmem_limit_bytes=40 * 1024 * 1024)

Z_GROUPS = [[y * NZ + z for z in range(NZ)] for y in range(NY)]
Y_GROUPS = [[y * NZ + z for y in range(NY)] for z in range(NZ)]


def in_hbm(array):
    return pltpu.with_memory_space_constraint(array, pltpu.HBM)


def shape(dims, dtype):
    return jax.ShapeDtypeStruct(dims, dtype)


def y_shift(array, by):
    pairs = [(y * NZ + z, (y + by) % NY * NZ + z) for y in range(NY) for z in range(NZ)]
    return lax.ppermute(array, "fsdp", pairs)


def gossip(array, distance):
    count = lax.axis_size("rep")
    return lax.ppermute(array, "rep", [(i, (i + distance) % count) for i in range(count)])


def lanes_of(rows):
    return lax.broadcasted_iota(jnp.int32, (rows, LANES), 1)


def flat_to_rows(flat, base, rows):
    lane = lanes_of(GROUPS)
    for j in range(8):
        if j == 0:
            part = flat[pl.ds(base, GROUPS, stride=7), :]
        else:
            part = flat[pl.ds(base + j - 1, GROUPS, stride=7), :]
            if j < 7:
                after = flat[pl.ds(base + j, GROUPS, stride=7), :]
                part = jnp.where(lane < LANES - 16 * j, after, part)
            part = pltpu.roll(part, 16 * j, 1)
        rows[pl.ds(j, GROUPS, stride=8), :] = jnp.where(lane < HEAD, part, 0.0)


def rows_to_flat(rows, base, flat):
    lane = lanes_of(GROUPS)
    for i in range(7):
        first = rows[pl.ds(base + i, GROUPS, stride=8), :]
        second = rows[pl.ds(base + i + 1, GROUPS, stride=8), :]
        if i:
            first = pltpu.roll(first, LANES - 16 * i, 1)
        second = pltpu.roll(second, HEAD - 16 * i, 1)
        flat[pl.ds(i, GROUPS, stride=7), :] = jnp.where(lane < HEAD - 16 * i, first, second)


def norm_kernel(parts, rows_in, place, tokens, cotangent, *refs):
    outs, refs = refs[:len(parts)], refs[len(parts):]
    values, cot, sems, out_sems, *nears = refs
    chunks = [pl.ds(i * CHUNK, CHUNK) for i in range(rows_in // CHUNK)]
    copies = [
        pltpu.make_async_copy(tokens.at[rows], values.at[rows], sems.at[i])
        for i, rows in enumerate(chunks)
    ]
    copies.append(
        pltpu.make_async_copy(cotangent.at[:, pl.ds(0, rows_in)], cot, sems.at[len(chunks)])
    )
    for copy in (copies[-1], *copies[:-1]):
        copy.start()
    copies[-1].wait()
    padded = jnp.concatenate([cot[...], jnp.zeros((LANES - HEAD, rows_in), BF16)], axis=0).T
    held = []
    for out, (k, first, count) in zip(outs, parts):
        held.append(nears.pop(0) if k else out)
        held[-1][:, QUARTER:] = padded[first:first + count]
    sent = []
    for i, rows in enumerate(chunks):
        copies[i].wait()
        totals = [jnp.zeros((CHUNK, LANES), F32) for _ in range(4)]
        for c in range(D // LANES):
            totals[c % 4] += values[rows, c * LANES:(c + 1) * LANES].astype(F32)
        center = jnp.sum(sum(totals), axis=-1, keepdims=True) * (1.0 / D)
        center = jnp.broadcast_to(center, (CHUNK, LANES))
        totals = [jnp.zeros((CHUNK, LANES), F32) for _ in range(2)]
        for c in range(D // LANES):
            apart = values[rows, c * LANES:(c + 1) * LANES].astype(F32) - center
            totals[c % 2] += apart * apart
        spread = jnp.sum(sum(totals), axis=-1, keepdims=True) * (1.0 / D)
        scale = jnp.broadcast_to(lax.rsqrt(spread + 1e-05), (CHUNK, LANES))
        for n, (k, first, count) in enumerate(parts):
            if not first <= i * CHUNK < first + count:
                continue
            into = pl.ds(i * CHUNK - first, CHUNK)
            start = (place[0] + k) % NY * QUARTER
            for c in range(QUARTER // LANES):
                lanes = pl.ds(pl.multiple_of(start + c * LANES, LANES), LANES)
                part = (values[rows, lanes].astype(F32) - center) * scale
                held[n][into, c * LANES:(c + 1) * LANES] = part.astype(BF16)
            if k:
                sent.append(
                    pltpu.make_async_copy(
                        held[n].at[into], outs[n].at[into], out_sems.at[n, i]
                    )
                )
                sent[-1].start()
    for copy in sent:
        copy.wait()


def norm(parts, rows_in, place, tokens, cotangent):
    return pl.pallas_call(
        functools.partial(norm_kernel, parts, rows_in),
        in_specs=[SMEM, HBM, HBM],
        out_specs=[HBM if k else VMEM for k, _, _ in parts],
        out_shape=[
            pltpu.HBM((count, BLOCK), BF16) if k else shape((count, BLOCK), BF16)
            for k, _, count in parts
        ],
        scratch_shapes=[
            pltpu.VMEM((rows_in, D), BF16),
            pltpu.VMEM((HEAD, rows_in), BF16),
            DMA((rows_in // CHUNK + 1,)),
            DMA((len(parts), rows_in // CHUNK)),
            *[pltpu.VMEM((count, BLOCK), BF16) for k, _, count in parts if k],
        ],
        compiler_params=PARAMS,
        name="norm",
    )(place, in_hbm(tokens), in_hbm(cotangent))


def start_kernel(mass, params, own, wire):
    own[:FLAT, :] = params[...]
    own[FLAT:, :] = jnp.full((WIRE - FLAT, LANES), mass[0], F32)
    wire[...] = (own[...] / mass[0]).astype(BF16)


def start(mass, params):
    return pl.pallas_call(
        start_kernel,
        in_specs=[SMEM, VMEM],
        out_specs=[VMEM] * 2,
        out_shape=[shape((WIRE, LANES), F32), shape((WIRE, LANES), BF16)],
        compiler_params=PARAMS,
        name="start",
    )(mass, params)


def preact_kernel(place, wires, *refs):
    blocks, (out, flat, rows, weights, held, sem) = refs[:len(PARTS)], refs[len(PARTS):]
    fetch = pltpu.make_async_copy(blocks[-1], held, sem)
    fetch.start()
    flat[...] = wires[...].astype(F32)
    for s in range(NZ):
        flat_to_rows(flat, s * WIRE, rows)
        weights[pl.ds(s * SHARD_ROWS, SHARD_ROWS), :] = rows[...].astype(BF16)
    for block, (k, first, count) in zip((*blocks[:-1], held), PARTS):
        if block is held:
            fetch.wait()
        product = jnp.dot(block[:, :QUARTER], weights[...], preferred_element_type=F32)
        start = pl.multiple_of((place[0] + NY - k) % NY * TOK + first, HALF)
        out[pl.ds(start, count), :] = product[:, :HEAD].astype(BF16)


def partial_preact(place, wires, blocks):
    return pl.pallas_call(
        preact_kernel,
        in_specs=[SMEM] + [VMEM] * len(PARTS) + [HBM],
        out_specs=VMEM,
        out_shape=shape((NY * TOK, HEAD), BF16),
        scratch_shapes=[
            pltpu.VMEM((NZ * WIRE, LANES), F32),
            pltpu.VMEM((SHARD_ROWS, LANES), F32),
            pltpu.VMEM((QUARTER, LANES), BF16),
            pltpu.VMEM((PARTS[-1][2], BLOCK), BF16),
            DMA,
        ],
        compiler_params=PARAMS,
        name="partial_preact",
    )(place, wires, *blocks[:-1], in_hbm(blocks[-1]))


def grad_kernel(near, place, partials, *refs):
    blocks, refs = refs[:len(PARTS)], refs[len(PARTS):]
    if near:
        states, (out, near_first, near_second, mixed), refs = refs[:4], refs[4:8], refs[8:]
        heads, rows, flat, held, near_peer, sems = refs
        pairs = [(blocks[-1], held), *zip(states, (near_first, near_second, mixed, near_peer))]
    else:
        out, heads, rows, flat, held, sems = refs
        pairs = [(blocks[-1], held)]
    copies = [
        pltpu.make_async_copy(source, into, sems.at[i]) for i, (source, into) in enumerate(pairs)
    ]
    for copy in copies:
        copy.start()
    heads[...] = jnp.zeros_like(heads)
    total = jnp.zeros((LANES, QUARTER), F32)
    for block, (k, first, count) in zip((*blocks[:-1], held), PARTS):
        start = pl.multiple_of((place[0] + NY - k) % NY * TOK + first, HALF)
        preact = jnp.zeros((count, HEAD), F32)
        for s in range(NY):
            preact = preact + partials[pl.ds(s * NY * TOK + start, count), :].astype(F32)
        if block is held:
            copies[0].wait()
        cot = block[:, QUARTER:QUARTER + HEAD].astype(F32)
        sig = 1.0 / (1.0 + jnp.exp(-preact))
        heads[:count, :HEAD] = (cot * sig * (1.0 + preact * (1.0 - sig))).astype(BF16)
        total = total + lax.dot_general(
            heads[:count], block[:, :QUARTER], (((0,), (0,)), ((), ())), preferred_element_type=F32
        )
    rows[...] = total.T
    flat[FLAT:, :] = jnp.zeros((WIRE - FLAT, LANES), F32)
    for s in range(NZ):
        rows_to_flat(rows, s * SHARD_ROWS, flat)
        out[s] = flat[...].astype(BF16)
    if near:
        for copy in copies[1:]:
            copy.wait()
        mixed[...] = 0.5 * (mixed[...] + near_peer[...])


def quarter_grad(place, partials, blocks, *states):
    near = bool(states)
    return pl.pallas_call(
        functools.partial(grad_kernel, near),
        in_specs=[SMEM] + [VMEM] * len(PARTS) + [HBM] * (1 + len(states)),
        out_specs=[VMEM] * (4 if near else 1),
        out_shape=[
            shape((NZ, WIRE, LANES), BF16),
            shape((FLAT, LANES), F32),
            shape((FLAT, LANES), F32),
            shape((WIRE, LANES), F32),
        ][:4 if near else 1],
        scratch_shapes=[
            pltpu.VMEM((TOK, LANES), BF16),
            pltpu.VMEM((QUARTER, LANES), F32),
            pltpu.VMEM((WIRE, LANES), F32),
            pltpu.VMEM((PARTS[-1][2], BLOCK), BF16),
            *[pltpu.VMEM((WIRE, LANES), F32)] * near,
            DMA((1 + len(states),)),
        ],
        compiler_params=PARAMS,
        name="quarter_grad",
    )(place, partials, *blocks[:-1], in_hbm(blocks[-1]), *map(in_hbm, states))


def adam(section, scales, terms, first_moment, second_moment, mixed):
    grads = terms[0].astype(F32)
    for s in range(1, NZ):
        grads = grads + terms[s].astype(F32)
    grads = grads[:FLAT, :]
    first = BETA_ONE * first_moment[...] + (1.0 - BETA_ONE) * grads
    second = BETA_TWO * second_moment[...] + (1.0 - BETA_TWO) * grads * grads
    update = first / scales[2 * section] / (jnp.sqrt(second / scales[2 * section + 1]) + ADAM_EPS)
    return first, second, mixed[:FLAT, :] - RATE * update, mixed[FLAT:, :]


def between_kernel(scales, terms, *refs):
    states, (far_first, far_second, new_own, wire), refs = refs[:4], refs[4:8], refs[8:]
    first_moment, second_moment, own, peer, new_first, new_second, sems = refs
    pairs = [
        *zip(states, (first_moment, second_moment, own, peer)),
        (new_first, far_first), (new_second, far_second),
    ]
    copies = [
        pltpu.make_async_copy(source, into, sems.at[i]) for i, (source, into) in enumerate(pairs)
    ]
    for copy in copies[:4]:
        copy.start()
    for copy in copies[:4]:
        copy.wait()
    own[...] = 0.5 * (own[...] + peer[...])
    first, second, params, mass = adam(0, scales, terms, first_moment, second_moment, own)
    new_first[...] = first
    new_second[...] = second
    for copy in copies[4:]:
        copy.start()
    new_own[:FLAT, :] = params
    new_own[FLAT:, :] = mass
    wire[...] = (new_own[...] / mass[0:1, :]).astype(BF16)
    for copy in copies[4:]:
        copy.wait()


def between(scales, terms, *states):
    flat, wide = pltpu.VMEM((FLAT, LANES), F32), pltpu.VMEM((WIRE, LANES), F32)
    return pl.pallas_call(
        between_kernel,
        in_specs=[SMEM, VMEM] + [HBM] * 4,
        out_specs=[HBM] * 2 + [VMEM] * 2,
        out_shape=[
            pltpu.HBM((FLAT, LANES), F32),
            pltpu.HBM((FLAT, LANES), F32),
            shape((WIRE, LANES), F32),
            shape((WIRE, LANES), BF16),
        ],
        scratch_shapes=[flat, flat, wide, wide, flat, flat, DMA((6,))],
        compiler_params=PARAMS,
        name="between",
    )(scales, terms, *map(in_hbm, states))


def last_kernel(scales, terms, first_moment, second_moment, mixed, *outs):
    new_params, new_first, new_second, new_mass = outs
    first, second, params, mass = adam(1, scales, terms, first_moment, second_moment, mixed)
    new_first[...] = first
    new_second[...] = second
    new_params[...] = params
    new_mass[0] = mass[0, 0]


def last(scales, *arrays):
    return pl.pallas_call(
        last_kernel,
        in_specs=[SMEM] + [VMEM] * 4,
        out_specs=[VMEM] * 3 + [SMEM],
        out_shape=[shape((FLAT, LANES), F32)] * 3 + [shape((1,), F32)],
        compiler_params=PARAMS,
        name="last",
    )(scales, *arrays)


def gather(array, groups):
    return lax.all_gather(array, "fsdp", axis=0, tiled=True, axis_index_groups=groups)


def gossip_alone(distance, own):
    return gossip(own, distance)


def gossip_beside(distance, own, wire):
    return gossip(own, distance), gather(wire, Z_GROUPS)


def at_level(pick, levels, function, *operands):
    return lax.switch(
        pick, [functools.partial(function, 2**level) for level in range(levels)], *operands
    )


def on_device(tokens, cotangent, params, first_moment, second_moment, mass, step_index):
    levels = lax.axis_size("rep").bit_length() - 1
    counts = (step_index[0] + 1 + jnp.arange(STEPS)).astype(F32)
    scales = jnp.stack(
        [1.0 - jnp.power(BETA_ONE, counts), 1.0 - jnp.power(BETA_TWO, counts)], axis=1
    ).reshape(-1)
    picks = [(step_index[0] + section) % levels for section in range(STEPS)]
    place = (lax.axis_index("fsdp") // NZ).astype(jnp.int32).reshape(1)
    first_moment = first_moment.reshape(FLAT, LANES)
    second_moment = second_moment.reshape(FLAT, LANES)
    own, wire = start(mass, params.reshape(FLAT, LANES))
    wire, scales, *picks = lax.optimization_barrier((wire, scales, *picks))
    blocks = {}
    for parts, rows_in in ((EARLY, HALF), (LATER, TOK)):
        for part, block in zip(parts, norm(parts, rows_in, place, tokens[0], cotangent[0].T)):
            blocks[part] = y_shift(block, part[0]) if part[0] else block
    blocks = [blocks[part] for part in PARTS]
    for section in range(STEPS):
        if section == 0:
            wires = gather(wire, Z_GROUPS)
            wires, own = lax.optimization_barrier((wires, own))
            peer = at_level(picks[section], levels, gossip_alone, own)
            wires, peer = lax.optimization_barrier((wires, peer))
        else:
            peer, wires = at_level(picks[section], levels, gossip_beside, own, wire)
        partials = gather(partial_preact(place, wires, blocks), Y_GROUPS)
        states = first_moment, second_moment, own, peer
        terms, *near = quarter_grad(place, partials, blocks, *(states if section else ()))
        terms = lax.all_to_all(terms, "fsdp", 0, 0, axis_index_groups=Z_GROUPS)
        terms, *picks = lax.optimization_barrier((terms, *picks))
        if section < STEPS - 1:
            first_moment, second_moment, own, wire = between(scales, terms, *states)
    *new, new_mass = last(scales, terms, *near)
    return tuple(array.reshape(1, -1) for array in new) + (new_mass,)


def solution(mesh):
    placed = (
        P("rep", "fsdp", None),
        P("rep", "fsdp", None),
        P("rep", "fsdp"),
        P("rep", "fsdp"),
        P("rep", "fsdp"),
        P("rep"),
        P(),
    )
    return jax.shard_map(
        on_device,
        mesh=mesh,
        in_specs=placed,
        out_specs=(P("rep", "fsdp"), P("rep", "fsdp"), P("rep", "fsdp"), P("rep")),
        check_vma=False,
    )
```

```python
import functools

import jax
import jax.numpy as jnp
from jax import lax
from jax.experimental import pallas as pl
from jax.experimental.pallas import tpu as pltpu
from jax.sharding import PartitionSpec as P

D = 7168
HEAD = 112
STEPS = 2
TOK = 256
NY = 4
NZ = 4
QUARTER = D // NY
SHARD_ROWS = QUARTER // NZ
LANES = 128
FLAT = SHARD_ROWS * HEAD // LANES
WIRE = FLAT + 8
GROUPS = SHARD_ROWS // 8
BLOCK = QUARTER + LANES
CHUNKS = 4
CHUNK = TOK // CHUNKS
HALF = TOK // 2
PARTS = ((0, 0, TOK), (1, 0, TOK), (2, 0, HALF), (2, HALF, HALF), (3, 0, TOK))

BETA_ONE = 0.9
BETA_TWO = 0.95
ADAM_EPS = 1e-08
RATE = 0.01

F32 = jnp.float32
BF16 = jnp.bfloat16
VMEM = pl.BlockSpec(memory_space=pltpu.VMEM)
SMEM = pl.BlockSpec(memory_space=pltpu.SMEM)
HBM = pl.BlockSpec(memory_space=pltpu.HBM)
DMA = pltpu.SemaphoreType.DMA
PARAMS = pltpu.CompilerParams(vmem_limit_bytes=40 * 1024 * 1024)

Z_GROUPS = [[y * NZ + z for z in range(NZ)] for y in range(NY)]
Y_GROUPS = [[y * NZ + z for y in range(NY)] for z in range(NZ)]


def in_hbm(array):
    return pltpu.with_memory_space_constraint(array, pltpu.HBM)


def shape(dims, dtype):
    return jax.ShapeDtypeStruct(dims, dtype)


def y_shift(array, by):
    pairs = [(y * NZ + z, (y + by) % NY * NZ + z) for y in range(NY) for z in range(NZ)]
    return lax.ppermute(array, "fsdp", pairs)


def gossip(array, distance):
    count = lax.axis_size("rep")
    return lax.ppermute(array, "rep", [(i, (i + distance) % count) for i in range(count)])


def lanes_of(rows):
    return lax.broadcasted_iota(jnp.int32, (rows, LANES), 1)


def flat_to_rows(flat, base, rows):
    lane = lanes_of(GROUPS)
    for j in range(8):
        if j == 0:
            part = flat[pl.ds(base, GROUPS, stride=7), :]
        else:
            part = flat[pl.ds(base + j - 1, GROUPS, stride=7), :]
            if j < 7:
                after = flat[pl.ds(base + j, GROUPS, stride=7), :]
                part = jnp.where(lane < LANES - 16 * j, after, part)
            part = pltpu.roll(part, 16 * j, 1)
        rows[pl.ds(j, GROUPS, stride=8), :] = jnp.where(lane < HEAD, part, 0.0)


def rows_to_flat(rows, base, flat):
    lane = lanes_of(GROUPS)
    for i in range(7):
        first = rows[pl.ds(base + i, GROUPS, stride=8), :]
        second = rows[pl.ds(base + i + 1, GROUPS, stride=8), :]
        if i:
            first = pltpu.roll(first, LANES - 16 * i, 1)
        second = pltpu.roll(second, HEAD - 16 * i, 1)
        flat[pl.ds(i, GROUPS, stride=7), :] = jnp.where(lane < HEAD - 16 * i, first, second)


def scaled(values, center, scale, out, width=QUARTER):
    for c in range(width // LANES):
        lanes = slice(c * LANES, (c + 1) * LANES)
        out[:, lanes] = ((values[:, lanes].astype(F32) - center) * scale).astype(BF16)


def padded_cotangent(cot):
    return jnp.concatenate([cot[...], jnp.zeros((LANES - HEAD, TOK), BF16)], axis=0).T


def norm_kernel(place, tokens, cotangent, *refs):
    outs, (centers, scales, values, cot, nears, sems, out_sems) = refs[:2], refs[2:]
    chunks = [pl.ds(i * CHUNK, CHUNK) for i in range(CHUNKS)]
    copies = [
        pltpu.make_async_copy(tokens.at[rows], values.at[rows], sems.at[i])
        for i, rows in enumerate(chunks)
    ]
    copies.append(pltpu.make_async_copy(cotangent, cot, sems.at[CHUNKS]))
    for copy in (copies[-1], *copies[:-1]):
        copy.start()
    copies[-1].wait()
    padded = padded_cotangent(cot)
    for n in range(2):
        nears[n, :, QUARTER:] = padded
    sent = []
    for i, rows in enumerate(chunks):
        copies[i].wait()
        totals = [jnp.zeros((CHUNK, LANES), F32) for _ in range(4)]
        for c in range(D // LANES):
            totals[c % 4] += values[rows, c * LANES:(c + 1) * LANES].astype(F32)
        center = jnp.sum(sum(totals), axis=-1, keepdims=True) * (1.0 / D)
        center = jnp.broadcast_to(center, (CHUNK, LANES))
        totals = [jnp.zeros((CHUNK, LANES), F32) for _ in range(2)]
        for c in range(D // LANES):
            apart = values[rows, c * LANES:(c + 1) * LANES].astype(F32) - center
            totals[c % 2] += apart * apart
        spread = jnp.sum(sum(totals), axis=-1, keepdims=True) * (1.0 / D)
        scale = jnp.broadcast_to(lax.rsqrt(spread + 1e-05), (CHUNK, LANES))
        centers[rows] = center
        scales[rows] = scale
        for n, k in enumerate((1, 3)):
            start = (place[0] + k) % NY * QUARTER
            for c in range(QUARTER // LANES):
                lanes = pl.ds(pl.multiple_of(start + c * LANES, LANES), LANES)
                part = (values[rows, lanes].astype(F32) - center) * scale
                nears[n, rows, c * LANES:(c + 1) * LANES] = part.astype(BF16)
            sent.append(
                pltpu.make_async_copy(nears.at[n, rows], outs[n].at[rows], out_sems.at[n, i])
            )
            sent[-1].start()
    for copy in sent:
        copy.wait()


def norm(place, tokens, cotangent):
    return pl.pallas_call(
        norm_kernel,
        in_specs=[SMEM, HBM, HBM],
        out_specs=[HBM] * 2 + [VMEM] * 2,
        out_shape=[pltpu.HBM((TOK, BLOCK), BF16)] * 2 + [shape((TOK, LANES), F32)] * 2,
        scratch_shapes=[
            pltpu.VMEM((TOK, D), BF16),
            pltpu.VMEM((HEAD, TOK), BF16),
            pltpu.VMEM((2, TOK, BLOCK), BF16),
            DMA((CHUNKS + 1,)),
            DMA((2, CHUNKS)),
        ],
        compiler_params=PARAMS,
        name="norm",
    )(place, in_hbm(tokens), in_hbm(cotangent))


def later_norm_kernel(place, tokens, cotangent, centers, scales, *refs):
    (own, *outs), (values, cot, nears, sems, out_sems) = refs[:3], refs[3:]
    halves = [pl.ds(h * HALF, HALF) for h in range(2)]
    copies = [pltpu.make_async_copy(cotangent, cot, sems.at[4])]
    for n, k in enumerate((2, 0)):
        start = pl.multiple_of((place[0] + k) % NY * QUARTER, LANES)
        for h, rows in enumerate(halves):
            copies.append(
                pltpu.make_async_copy(
                    tokens.at[rows, pl.ds(start, QUARTER)], values.at[n, rows], sems.at[2 * n + h]
                )
            )
    for copy in copies:
        copy.start()
    copies[0].wait()
    padded = padded_cotangent(cot)
    own[:, QUARTER:] = padded
    sent = []
    for h, rows in enumerate(halves):
        nears[h, :, QUARTER:] = padded[h * HALF:(h + 1) * HALF]
        copies[1 + h].wait()
        scaled(values.at[0, rows], centers[rows], scales[rows], nears.at[h])
        sent.append(pltpu.make_async_copy(nears.at[h], outs[h], out_sems.at[h]))
        sent[-1].start()
    for h, rows in enumerate(halves):
        copies[3 + h].wait()
        scaled(values.at[1, rows], centers[rows], scales[rows], own.at[rows])
    for copy in sent:
        copy.wait()


def later_norm(place, tokens, cotangent, centers, scales):
    return pl.pallas_call(
        later_norm_kernel,
        in_specs=[SMEM, HBM, HBM, VMEM, VMEM],
        out_specs=[VMEM] + [HBM] * 2,
        out_shape=[shape((TOK, BLOCK), BF16)] + [pltpu.HBM((HALF, BLOCK), BF16)] * 2,
        scratch_shapes=[
            pltpu.VMEM((2, TOK, QUARTER), BF16),
            pltpu.VMEM((HEAD, TOK), BF16),
            pltpu.VMEM((2, HALF, BLOCK), BF16),
            DMA((5,)),
            DMA((2,)),
        ],
        compiler_params=PARAMS,
        name="later_norm",
    )(place, in_hbm(tokens), in_hbm(cotangent), centers, scales)


def start_kernel(mass, params, own, wire):
    own[:FLAT, :] = params[...]
    own[FLAT:, :] = jnp.full((WIRE - FLAT, LANES), mass[0], F32)
    wire[...] = (own[...] / mass[0]).astype(BF16)


def start(mass, params):
    return pl.pallas_call(
        start_kernel,
        in_specs=[SMEM, VMEM],
        out_specs=[VMEM] * 2,
        out_shape=[shape((WIRE, LANES), F32), shape((WIRE, LANES), BF16)],
        compiler_params=PARAMS,
        name="start",
    )(mass, params)


def preact_kernel(place, wires, *refs):
    blocks, (out, flat, rows, weights, held, sem) = refs[:len(PARTS)], refs[len(PARTS):]
    fetch = pltpu.make_async_copy(blocks[-1], held, sem)
    fetch.start()
    flat[...] = wires[...].astype(F32)
    for s in range(NZ):
        flat_to_rows(flat, s * WIRE, rows)
        weights[pl.ds(s * SHARD_ROWS, SHARD_ROWS), :] = rows[:SHARD_ROWS, :].astype(BF16)
    for block, (k, first, count) in zip((*blocks[:-1], held), PARTS):
        if block is held:
            fetch.wait()
        product = jnp.dot(block[:, :QUARTER], weights[...], preferred_element_type=F32)
        start = pl.multiple_of((place[0] + NY - k) % NY * TOK + first, HALF)
        out[pl.ds(start, count), :] = product[:, :HEAD].astype(BF16)


def partial_preact(place, wires, blocks):
    return pl.pallas_call(
        preact_kernel,
        in_specs=[SMEM] + [VMEM] * len(PARTS) + [HBM],
        out_specs=VMEM,
        out_shape=shape((NY * TOK, HEAD), BF16),
        scratch_shapes=[
            pltpu.VMEM((NZ * WIRE, LANES), F32),
            pltpu.VMEM((SHARD_ROWS + 8, LANES), F32),
            pltpu.VMEM((QUARTER, LANES), BF16),
            pltpu.VMEM((PARTS[-1][2], BLOCK), BF16),
            DMA,
        ],
        compiler_params=PARAMS,
        name="partial_preact",
    )(place, wires, *blocks[:-1], in_hbm(blocks[-1]))


def grad_kernel(near, place, partials, *refs):
    blocks, refs = refs[:len(PARTS)], refs[len(PARTS):]
    if near:
        states, (out, near_first, near_second, mixed), refs = refs[:4], refs[4:8], refs[8:]
        heads, rows, flat, held, near_peer, sems = refs
        pairs = [(blocks[-1], held), *zip(states, (near_first, near_second, mixed, near_peer))]
    else:
        out, heads, rows, flat, held, sems = refs
        pairs = [(blocks[-1], held)]
    copies = [
        pltpu.make_async_copy(source, into, sems.at[i]) for i, (source, into) in enumerate(pairs)
    ]
    for copy in copies:
        copy.start()
    heads[...] = jnp.zeros_like(heads)
    total = jnp.zeros((LANES, QUARTER), F32)
    for block, (k, first, count) in zip((*blocks[:-1], held), PARTS):
        start = pl.multiple_of((place[0] + NY - k) % NY * TOK + first, HALF)
        preact = jnp.zeros((count, HEAD), F32)
        for s in range(NY):
            preact = preact + partials[pl.ds(s * NY * TOK + start, count), :].astype(F32)
        if block is held:
            copies[0].wait()
        cot = block[:, QUARTER:QUARTER + HEAD].astype(F32)
        sig = 1.0 / (1.0 + jnp.exp(-preact))
        heads[:count, :HEAD] = (cot * sig * (1.0 + preact * (1.0 - sig))).astype(BF16)
        total = total + lax.dot_general(
            heads[:count], block[:, :QUARTER], (((0,), (0,)), ((), ())), preferred_element_type=F32
        )
    rows[:QUARTER, :] = total.T
    flat[FLAT:, :] = jnp.zeros((WIRE - FLAT, LANES), F32)
    for s in range(NZ):
        rows_to_flat(rows, s * SHARD_ROWS, flat)
        out[s] = flat[...].astype(BF16)
    if near:
        for copy in copies[1:]:
            copy.wait()
        mixed[...] = 0.5 * (mixed[...] + near_peer[...])


def quarter_grad(place, partials, blocks, *states):
    near = bool(states)
    return pl.pallas_call(
        functools.partial(grad_kernel, near),
        in_specs=[SMEM] + [VMEM] * len(PARTS) + [HBM] * (1 + len(states)),
        out_specs=[VMEM] * (4 if near else 1),
        out_shape=[
            shape((NZ, WIRE, LANES), BF16),
            shape((FLAT, LANES), F32),
            shape((FLAT, LANES), F32),
            shape((WIRE, LANES), F32),
        ][:4 if near else 1],
        scratch_shapes=[
            pltpu.VMEM((TOK, LANES), BF16),
            pltpu.VMEM((QUARTER + 8, LANES), F32),
            pltpu.VMEM((WIRE, LANES), F32),
            pltpu.VMEM((PARTS[-1][2], BLOCK), BF16),
            *[pltpu.VMEM((WIRE, LANES), F32)] * near,
            DMA((1 + len(states),)),
        ],
        compiler_params=PARAMS,
        name="quarter_grad",
    )(place, partials, *blocks[:-1], in_hbm(blocks[-1]), *map(in_hbm, states))


def summed(terms):
    grads = terms[0].astype(F32)
    for s in range(1, NZ):
        grads = grads + terms[s].astype(F32)
    return grads[:FLAT, :]


def adam(section, scales, grads, first_moment, second_moment, mixed):
    first = BETA_ONE * first_moment[...] + (1.0 - BETA_ONE) * grads
    second = BETA_TWO * second_moment[...] + (1.0 - BETA_TWO) * grads * grads
    update = first / scales[2 * section] / (jnp.sqrt(second / scales[2 * section + 1]) + ADAM_EPS)
    return first, second, mixed[:FLAT, :] - RATE * update, mixed[FLAT:, :]


def between_kernel(scales, terms, *refs):
    states, (far_first, far_second, new_own, wire), refs = refs[:4], refs[4:8], refs[8:]
    first_moment, second_moment, own, peer, new_first, new_second, sems = refs
    pairs = [
        *zip(states, (first_moment, second_moment, own, peer)),
        (new_first, far_first), (new_second, far_second),
    ]
    copies = [
        pltpu.make_async_copy(source, into, sems.at[i]) for i, (source, into) in enumerate(pairs)
    ]
    for copy in copies[:4]:
        copy.start()
    grads = summed(terms)
    for copy in copies[:4]:
        copy.wait()
    own[...] = 0.5 * (own[...] + peer[...])
    first, second, params, mass = adam(0, scales, grads, first_moment, second_moment, own)
    new_first[...] = first
    new_second[...] = second
    for copy in copies[4:]:
        copy.start()
    new_own[:FLAT, :] = params
    new_own[FLAT:, :] = mass
    wire[...] = (new_own[...] / mass[0:1, :]).astype(BF16)
    for copy in copies[4:]:
        copy.wait()


def between(scales, terms, *states):
    flat, wide = pltpu.VMEM((FLAT, LANES), F32), pltpu.VMEM((WIRE, LANES), F32)
    return pl.pallas_call(
        between_kernel,
        in_specs=[SMEM, VMEM] + [HBM] * 4,
        out_specs=[HBM] * 2 + [VMEM] * 2,
        out_shape=[
            pltpu.HBM((FLAT, LANES), F32),
            pltpu.HBM((FLAT, LANES), F32),
            shape((WIRE, LANES), F32),
            shape((WIRE, LANES), BF16),
        ],
        scratch_shapes=[flat, flat, wide, wide, flat, flat, DMA((6,))],
        compiler_params=PARAMS,
        name="between",
    )(scales, terms, *map(in_hbm, states))


def last_kernel(scales, terms, first_moment, second_moment, mixed, *outs):
    new_params, new_first, new_second, new_mass = outs
    first, second, params, mass = adam(1, scales, summed(terms), first_moment, second_moment, mixed)
    new_first[...] = first
    new_second[...] = second
    new_params[...] = params
    new_mass[0] = mass[0, 0]


def last(scales, *arrays):
    return pl.pallas_call(
        last_kernel,
        in_specs=[SMEM] + [VMEM] * 4,
        out_specs=[VMEM] * 3 + [SMEM],
        out_shape=[shape((FLAT, LANES), F32)] * 3 + [shape((1,), F32)],
        compiler_params=PARAMS,
        name="last",
    )(scales, *arrays)


def gather(array, groups):
    return lax.all_gather(array, "fsdp", axis=0, tiled=True, axis_index_groups=groups)


def gossip_alone(distance, own):
    return gossip(own, distance)


def gossip_beside(distance, own, wire):
    return gossip(own, distance), gather(wire, Z_GROUPS)


def at_level(pick, levels, function, *operands):
    return lax.switch(
        pick, [functools.partial(function, 2**level) for level in range(levels)], *operands
    )


def on_device(tokens, cotangent, params, first_moment, second_moment, mass, step_index):
    levels = lax.axis_size("rep").bit_length() - 1
    counts = (step_index[0] + 1 + jnp.arange(STEPS)).astype(F32)
    scales = jnp.stack(
        [1.0 - jnp.power(BETA_ONE, counts), 1.0 - jnp.power(BETA_TWO, counts)], axis=1
    ).reshape(-1)
    picks = [(step_index[0] + section) % levels for section in range(STEPS)]
    place = (lax.axis_index("fsdp") // NZ).astype(jnp.int32).reshape(1)
    first_moment = first_moment.reshape(FLAT, LANES)
    second_moment = second_moment.reshape(FLAT, LANES)
    own, wire = start(mass, params.reshape(FLAT, LANES))
    wire, scales, *picks = lax.optimization_barrier((wire, scales, *picks))
    one, three, *stats = norm(place, tokens[0], cotangent[0].T)
    own_block, *two = later_norm(place, tokens[0], cotangent[0].T, *stats)
    blocks = [own_block, one, *two, three]
    blocks = [y_shift(block, part[0]) if part[0] else block for block, part in zip(blocks, PARTS)]
    for section in range(STEPS):
        if section == 0:
            wires = gather(wire, Z_GROUPS)
            wires, own = lax.optimization_barrier((wires, own))
            peer = at_level(picks[section], levels, gossip_alone, own)
            wires, peer = lax.optimization_barrier((wires, peer))
        else:
            peer, wires = at_level(picks[section], levels, gossip_beside, own, wire)
        partials = gather(partial_preact(place, wires, blocks), Y_GROUPS)
        states = first_moment, second_moment, own, peer
        terms, *near = quarter_grad(place, partials, blocks, *(states if section else ()))
        terms = lax.all_to_all(terms, "fsdp", 0, 0, axis_index_groups=Z_GROUPS)
        terms, *picks = lax.optimization_barrier((terms, *picks))
        if section < STEPS - 1:
            first_moment, second_moment, own, wire = between(scales, terms, *states)
    *new, new_mass = last(scales, terms, *near)
    return tuple(array.reshape(1, -1) for array in new) + (new_mass,)


def solution(mesh):
    placed = (
        P("rep", "fsdp", None),
        P("rep", "fsdp", None),
        P("rep", "fsdp"),
        P("rep", "fsdp"),
        P("rep", "fsdp"),
        P("rep"),
        P(),
    )
    return jax.shard_map(
        on_device,
        mesh=mesh,
        in_specs=placed,
        out_specs=(P("rep", "fsdp"), P("rep", "fsdp"), P("rep", "fsdp"), P("rep")),
        check_vma=False,
    )
```
